32 devices in a mesh: sa: 8 (over z, core), sb: 4 (over y, x).
Axes of the slice: x: 2, y: 2, z: 4, core: 2. Of those that a mesh axis runs over, the one named last changes fastest.
Arguments:
- queries: bfloat16 [4096, 16, 192], P(('sa', 'sb')), may hold values from -110 to 110
- keys: bfloat16 [4096, 192], P(('sa', 'sb')), may hold values from -6 to 6
- values: bfloat16 [4096, 128], P(('sa', 'sb')), may hold values from -6 to 6
- key_first: bfloat16 [6144, 192], replicated, may hold values from -0.078125 to 0.078125
- key_second: bfloat16 [192, 192], replicated, may hold values from -0.4375 to 0.4375
- value_first: bfloat16 [4096, 128], replicated, may hold values from -0.09375 to 0.09375
- value_second: bfloat16 [128, 128], replicated, may hold values from -0.5 to 0.5
- gate_table: float32 [16, 2], replicated, may hold values from 0.1 to 1
- gate_index: int32 [4096, 16], P(('sa', 'sb')), may hold values from 0 to 15
Outputs:
- mixed: bfloat16 [4096, 16, 128], P(('sa', 'sb'))
The draws below stay inside these ranges and needn't reach their ends.
All inputs are finite; a program needn't handle non-finite values.
Results may differ from the reference program's by a relative error of at most 0.0053.
Values may be sent and summed in bfloat16 or wider, within the bound.
A program may use at most 64 MiB of HBM per device.

```python
import jax
import jax.numpy as jnp
from jax import lax

HEADS = 16
DK = 192
DV = 128
BLOCK = 32
STRIDE = 16
WINDOW = 512
LEVELS = 16
TOKENS = 4096
NB = 256


def draw_queries(key, part):
    first = jax.random.fold_in(jax.random.fold_in(key, 11), 0)
    base = 4.0 * jax.random.truncated_normal(first, -6.0, 6.0, (TOKENS, HEADS, DK), jnp.float32)
    return base.astype(jnp.bfloat16)


def touch_ends(array, stream_key, smallest, high):
    spot = [jax.random.randint(jax.random.fold_in(stream_key, axis), (), 0, length) for axis, length in enumerate(array.shape)]
    longest = array.shape.index(max(array.shape))
    neighbour = spot[:longest] + [(spot[longest] + 1) % array.shape[longest]] + spot[longest + 1:]
    return array.at[tuple(spot)].set(smallest).at[tuple(neighbour)].set(high)


def block_levels(stream_key, shape, cuts, smallest, top_value):
    factor_of, own = 1.0, jax.random.fold_in(stream_key, 6)
    for position, parts in cuts:
        heights = jnp.exp(jax.random.uniform(jax.random.fold_in(own, position), (parts,), jnp.float32, smallest / len(cuts), top_value / len(cuts)))
        factor_of = factor_of * jnp.repeat(heights, shape[position] // parts).reshape([-1 if axis == position else 1 for axis in range(len(shape))])
    return factor_of


def gaussian(stream_key, shape, scale, most, cuts=(), kind=jnp.bfloat16):
    values = jax.random.normal(stream_key, shape, jnp.float32) * scale
    if len(cuts) > 0:
        values = block_levels(stream_key, shape, cuts, -0.22, 0.18) * values
    return jnp.clip(values, min=-most, max=most).astype(kind)


def setup_inputs(seed: int = 0) -> dict:
    key_of = jax.random.split(jax.random.key(seed), 10)
    return {
        "queries": draw_queries(jax.random.fold_in(key_of[9], 71), 0),
        "keys": gaussian(key_of[1], (TOKENS, DK), 1.0, 6.0, ((0, 32),)),
        "values": gaussian(key_of[2], (TOKENS, DV), 1.0, 6.0, ((0, 32),)),
        "key_first": gaussian(key_of[3], (BLOCK * DK, DK), (BLOCK * DK) ** -0.5, 0.078125),
        "key_second": gaussian(key_of[4], (DK, DK), DK ** -0.5, 0.4375),
        "value_first": gaussian(key_of[5], (BLOCK * DV, DV), (BLOCK * DV) ** -0.5, 0.09375),
        "value_second": gaussian(key_of[6], (DV, DV), DV ** -0.5, 0.5),
        "gate_table": jnp.clip(jax.random.uniform(key_of[7], (LEVELS, 2), jnp.float32, 0.1, 1.0), 0.1, 1.0),
        "gate_index": touch_ends(jax.random.randint(key_of[8], (TOKENS, HEADS), 0, LEVELS), jax.random.fold_in(key_of[8], 1), 0, LEVELS - 1).astype(jnp.int32),
    }


def compress(rows, first, second):
    width = rows.shape[1]
    padded = jnp.concatenate([jnp.zeros((STRIDE, width), rows.dtype), rows], axis=0)
    front = padded[:TOKENS].reshape(NB, STRIDE * width)
    back = padded[STRIDE:].reshape(NB, STRIDE * width)
    flat = jnp.concatenate([front, back], axis=1)
    hidden = jax.nn.silu(jnp.dot(flat, first, preferred_element_type=jnp.float32)).astype(jnp.bfloat16)
    return jnp.dot(hidden, second, preferred_element_type=jnp.float32).astype(jnp.bfloat16)


def reference(queries, keys, values, key_first, key_second, value_first, value_second, gate_table, gate_index):
    summary_keys = compress(keys, key_first, key_second)
    summary_values = compress(values, value_first, value_second)
    scale = DK ** -0.5
    span = 512
    key_pad = jnp.concatenate([jnp.zeros((WINDOW, DK), keys.dtype), keys], axis=0)
    value_pad = jnp.concatenate([jnp.zeros((WINDOW, DV), values.dtype), values], axis=0)
    block_ends = STRIDE * lax.iota(jnp.int32, NB) + STRIDE - 1

    def one_block(index):
        begin = (index * span).astype(jnp.int32)
        query_rows = lax.dynamic_slice_in_dim(queries, begin, span, 0).reshape(span * HEADS, DK)
        positions = begin + lax.iota(jnp.int32, span * HEADS) // HEADS
        scores = jnp.dot(query_rows, summary_keys.T, preferred_element_type=jnp.float32) * scale
        visible = block_ends[None, :] <= positions[:, None]
        masked = jnp.where(visible, scores, -1e30)
        top = jnp.max(masked, axis=1, keepdims=True)
        weights = jnp.where(visible, jnp.exp(masked - top), 0.0)
        total = jnp.sum(weights, axis=1)
        numer = jnp.dot(weights.astype(jnp.bfloat16), summary_values, preferred_element_type=jnp.float32)
        present = total > 0.0
        compressed = jnp.where(present[:, None], numer / jnp.where(present, total, 1.0)[:, None], 0.0)
        near_keys = lax.dynamic_slice_in_dim(key_pad, begin, span + WINDOW, 0)
        near_values = lax.dynamic_slice_in_dim(value_pad, begin, span + WINDOW, 0)
        key_pos = begin - WINDOW + lax.iota(jnp.int32, span + WINDOW)
        near_scores = jnp.dot(query_rows, near_keys.T, preferred_element_type=jnp.float32) * scale
        inside = (key_pos[None, :] <= positions[:, None]) & (key_pos[None, :] > positions[:, None] - WINDOW) & (key_pos[None, :] >= 0)
        near_masked = jnp.where(inside, near_scores, -1e30)
        near_top = jnp.max(near_masked, axis=1, keepdims=True)
        near_weights = jnp.where(inside, jnp.exp(near_masked - near_top), 0.0)
        near_total = jnp.sum(near_weights, axis=1)
        window = jnp.dot(near_weights.astype(jnp.bfloat16), near_values, preferred_element_type=jnp.float32) / near_total[:, None]
        chosen = lax.dynamic_slice_in_dim(gate_index, begin, span, 0).reshape(span * HEADS)
        onehot = (chosen[:, None] == lax.iota(jnp.int32, LEVELS)[None, :]).astype(jnp.float32)
        gates = jnp.sum(onehot[:, :, None] * gate_table[None, :, :], axis=1)
        mixed = gates[:, 0:1] * compressed + gates[:, 1:2] * window
        return mixed.astype(jnp.bfloat16).reshape(span, HEADS, DV)

    result = lax.map(one_block, jnp.arange(TOKENS // span, dtype=jnp.int32))
    return result.reshape(TOKENS, HEADS, DV)
```

```python
import functools

import jax
import jax.numpy as jnp
from jax import lax
from jax.experimental import pallas as pl
from jax.experimental.pallas import tpu as pltpu
from jax.sharding import PartitionSpec as P

STRIDE = 16
WINDOW = 512
EXTRA = 16
NEG = -1e30
F32 = jnp.float32
BF16 = jnp.bfloat16


def dot(a, b):
    return jnp.dot(a, b, preferred_element_type=F32)


def silu(x):
    return x / (1.0 + jnp.exp(-x))


def kernel(
    n,
    inner,
    group,
    q_hbm,
    kt_ref,
    v_ref,
    w1k_hbm,
    w2k_ref,
    w1v_hbm,
    w2v_ref,
    table_ref,
    index_ref,
    out_ref,
    q_buf,
    w1k_buf,
    w1v_buf,
    kbuf,
    vbuf,
    gath,
    krows,
    vcols,
    crows,
    ccols,
    near,
    gates,
    out32,
    load_sem,
    halo_send,
    halo_recv,
    sum_send,
    sum_recv,
):
    heads, depth, rows = q_hbm.shape
    dv = v_ref.shape[1]
    reach = WINDOW // rows
    count = rows // STRIDE
    chunk = group * count
    chunks = n // group
    me = lax.axis_index("sa") * inner + lax.axis_index("sb")
    factor = depth ** (-0.5) * 1.4426950408889634

    def place(i):
        return (i // inner, i % inner)

    loads = [
        pltpu.make_async_copy(w1k_hbm, w1k_buf, load_sem.at[0]),
        pltpu.make_async_copy(w1v_hbm, w1v_buf, load_sem.at[1]),
        pltpu.make_async_copy(q_hbm, q_buf.at[:, pl.ds(0, depth), :], load_sem.at[2]),
    ]
    for load in loads:
        load.start()

    barrier = pltpu.get_barrier_semaphore()

    @pl.loop(0, me)
    def _(i):
        pl.semaphore_signal(
            barrier, inc=1, device_id=place(i), device_id_type=pl.DeviceIdType.MESH
        )

    token = lax.broadcasted_iota(jnp.int32, (EXTRA, rows), 1)
    line = lax.broadcasted_iota(jnp.int32, (EXTRA, rows), 0)
    marks = jnp.where((line == 0) | (line - 1 == (token + 1) // STRIDE), 1.0, 0.0).astype(BF16)
    for h in range(heads):
        q_buf[h, depth:, :] = marks
    for i in range(1, reach + 1):

        @pl.when(me < i)
        def _():
            kbuf[i - 1] = jnp.zeros(kbuf.shape[1:], BF16)
            vbuf[i - 1] = jnp.zeros(vbuf.shape[1:], BF16)

    index = index_ref[...]
    for column in range(2):
        gate = jnp.zeros(index.shape, F32)
        for level in range(table_ref.shape[1]):
            gate = jnp.where(index == level, table_ref[column, level], gate)
        gates[column] = gate

    @pl.when(me < n - 1)
    def _():
        pl.semaphore_wait(barrier, n - 1 - me)

    def halo(i):
        to = jnp.minimum(me + i, n - 1)
        return [
            pltpu.make_async_remote_copy(
                src_ref=src,
                dst_ref=dst.at[i - 1],
                send_sem=halo_send.at[part, i - 1],
                recv_sem=halo_recv.at[part, i - 1],
                device_id=place(to),
                device_id_type=pl.DeviceIdType.MESH,
            )
            for part, (src, dst) in enumerate([(kt_ref, kbuf), (v_ref, vbuf)])
        ]

    for i in range(1, reach + 1):

        @pl.when(me + i < n)
        def _():
            for copy in halo(i):
                copy.start()

    @pl.when(me >= 1)
    def _():
        for copy in halo(1):
            copy.wait_recv()

    loads[0].wait()
    own_k = kt_ref[...]
    own_v = v_ref[...]
    lane = lax.broadcasted_iota(jnp.int32, (depth, rows), 1)
    merged = jnp.where(lane >= rows - STRIDE, kbuf[0].astype(F32), own_k.astype(F32))
    front_k = pltpu.roll(merged, STRIDE, 1).astype(BF16)
    zero_k = jnp.zeros_like(own_k)
    spread = [
        jnp.where(lane % STRIDE == u, part, zero_k)
        for part in (front_k, own_k)
        for u in range(STRIDE)
    ]
    sums = dot(w1k_buf[...], jnp.concatenate(spread, axis=0))
    hidden = jnp.sum(sums.T.reshape(count, STRIDE, depth), axis=1)
    key_summary = dot(silu(hidden).astype(BF16), w2k_ref[...])

    loads[1].wait()
    line = lax.broadcasted_iota(jnp.int32, (rows, dv), 0)
    front_v = jnp.concatenate([vbuf[0, rows - STRIDE :, :], own_v[: rows - STRIDE]], axis=0)
    zero_v = jnp.zeros_like(own_v)
    spread = [
        jnp.where(line % STRIDE == u, part, zero_v)
        for part in (front_v, own_v)
        for u in range(STRIDE)
    ]
    sums = dot(jnp.concatenate(spread, axis=1), w1v_buf[...])
    hidden = jnp.sum(sums.reshape(count, STRIDE, dv), axis=1)
    value_summary = dot(silu(hidden).astype(BF16), w2v_ref[...])
    wide = gath.shape[2]
    top = jnp.concatenate([key_summary, jnp.zeros((count, wide - depth), F32)], axis=1)
    bottom = jnp.concatenate([value_summary, jnp.zeros((count, wide - dv), F32)], axis=1)
    gath[me] = jnp.concatenate([top, bottom], axis=0).astype(BF16)

    def summary(source, to):
        return pltpu.make_async_remote_copy(
            src_ref=gath.at[source],
            dst_ref=gath.at[source],
            send_sem=sum_send.at[to],
            recv_sem=sum_recv.at[source],
            device_id=place(to),
            device_id_type=pl.DeviceIdType.MESH,
        )

    @pl.loop(me + 1, n)
    def _(to):
        summary(me, to).start()

    for i in range(2, reach + 1):

        @pl.when(me >= i)
        def _():
            for copy in halo(i):
                copy.wait_recv()

    first_lane = lax.broadcasted_iota(jnp.int32, (rows, EXTRA), 1) == 0
    for slot in range(reach + 1):
        i = reach - slot
        kt = own_k if i == 0 else kbuf[i - 1]
        vv = own_v if i == 0 else vbuf[i - 1]
        here = pl.ds(slot * rows, rows)
        krows[here, :depth] = kt.astype(F32).T.astype(BF16)
        krows[here, depth:] = jnp.where(first_lane & (me < i), NEG, 0.0).astype(BF16)
        vcols[:dv, here] = vv.astype(F32).T.astype(BF16)
    vcols[dv:, :] = jnp.ones((EXTRA, vcols.shape[1]), BF16)
    loads[2].wait()
    pair = 2 * rows
    within = lax.broadcasted_iota(jnp.int32, (rows, pair), 0) <= (
        lax.broadcasted_iota(jnp.int32, (rows, pair), 1) % rows
    )

    def queries(h):
        return jnp.concatenate([q_buf[2 * h], q_buf[2 * h + 1]], axis=1)

    @pl.loop(0, heads // 2)
    def _(h):
        scores = dot(krows[...], queries(h))
        edge = jnp.where(within, scores[reach * rows :], scores[:rows])
        kept = jnp.concatenate([edge, scores[rows : reach * rows]], axis=0)
        best = jnp.max(kept, axis=0, keepdims=True)
        weights = jnp.exp2(kept * factor - best * factor)
        old = jnp.where(within, 0.0, weights[:rows])
        new = jnp.where(within, weights[:rows], 0.0)
        full = jnp.concatenate([old, weights[rows:], new], axis=0).astype(BF16)
        near[h] = dot(vcols[...], full)

    @pl.loop(0, me)
    def _(source):
        summary(source, me).wait_recv()

    needed = me // group + 1

    def prepare(c, carry):
        whole = gath[pl.ds(c * group, group)].astype(F32)
        device = c * group + lax.broadcasted_iota(jnp.int32, (group, 2 * count, wide), 0)
        whole = jnp.where(device <= me, whole, 0.0)
        block = c * chunk + lax.broadcasted_iota(jnp.int32, (chunk, EXTRA), 0)
        column = lax.broadcasted_iota(jnp.int32, (chunk, EXTRA), 1)
        local = block - me * count
        hide = ((column == 0) & (local >= count)) | (
            (column >= 1) & (local >= 0) & (column - 1 <= local)
        )
        here = pl.ds(pl.multiple_of(c * chunk, chunk), chunk)
        crows[here, :depth] = whole[:, :count, :depth].reshape(chunk, depth).astype(BF16)
        crows[here, depth:] = jnp.where(hide, NEG, 0.0).astype(BF16)
        ccols[c, :dv, :] = whole[:, count:, :dv].reshape(chunk, dv).T.astype(BF16)
        ccols[c, dv:, :] = jnp.ones((EXTRA, chunk), BF16)
        return carry

    if chunks == 1:
        prepare(0, 0)
    else:
        lax.fori_loop(0, needed, prepare, 0)

    @pl.loop(0, heads // 2)
    def _(h):
        query = queries(h)

        def part(c):
            here = pl.ds(pl.multiple_of(c * chunk, chunk), chunk)
            scores = dot(crows[here, :], query)
            return scores, jnp.max(scores, axis=0, keepdims=True)

        def weigh(c, scores, best):
            return dot(ccols[c], jnp.exp2(scores * factor - best * factor).astype(BF16))

        if chunks == 1:
            scores, best = part(0)
            far = weigh(0, scores, jnp.maximum(best, 0.1 * NEG))
        else:

            def absorb(c, carry):
                best, total = carry
                scores, fresh = part(c)
                fresh = jnp.maximum(best, fresh)
                shrink = jnp.exp2(best * factor - fresh * factor)
                return fresh, total * shrink + weigh(c, scores, fresh)

            start = (jnp.full((1, pair), 0.1 * NEG, F32), jnp.zeros((dv + EXTRA, pair), F32))
            far = lax.fori_loop(0, needed, absorb, start)[1]
        local = near[h]
        gate = [
            jnp.concatenate([gates[c, pl.ds(2 * h, 1), :], gates[c, pl.ds(2 * h + 1, 1), :]], axis=1)
            for c in range(2)
        ]
        total = far[dv : dv + 1]
        seen = total > 0.0
        far_gate = jnp.where(seen, gate[0] / jnp.where(seen, total, 1.0), 0.0)
        near_gate = gate[1] / local[dv : dv + 1]
        mixed = far[:dv] * far_gate + local[:dv] * near_gate
        for side in range(2):
            out32[pl.ds(2 * h + side, rows, stride=heads), :] = mixed[
                :, side * rows : (side + 1) * rows
            ].T

    out_ref[...] = out32[...].reshape(rows, heads, dv).astype(BF16)

    for i in range(1, reach + 1):

        @pl.when(me + i < n)
        def _():
            for copy in halo(i):
                copy.wait_send()

    @pl.loop(me + 1, n)
    def _(to):
        summary(me, to).wait_send()


def local(
    n,
    inner,
    queries,
    keys,
    values,
    key_first,
    key_second,
    value_first,
    value_second,
    gate_table,
    gate_index,
):
    rows, heads, depth = queries.shape
    dv = values.shape[1]
    reach = WINDOW // rows
    count = rows // STRIDE
    group = min(n, 256 // count)
    chunk = group * count
    wide = 256
    flops = 2 * rows * heads * (depth + dv) * (WINDOW + rows + n * count)
    vmem = pl.BlockSpec(memory_space=pltpu.VMEM)
    hbm = pl.BlockSpec(memory_space=pltpu.HBM)
    smem = pl.BlockSpec(memory_space=pltpu.SMEM)
    return pl.pallas_call(
        functools.partial(kernel, n, inner, group),
        out_shape=jax.ShapeDtypeStruct((rows, heads, dv), BF16),
        in_specs=[hbm, vmem, vmem, hbm, vmem, hbm, vmem, smem, vmem],
        out_specs=vmem,
        scratch_shapes=[
            pltpu.VMEM((heads, depth + EXTRA, rows), BF16),
            pltpu.VMEM(key_first.shape[::-1], BF16),
            pltpu.VMEM(value_first.shape, BF16),
            pltpu.VMEM((reach, depth, rows), BF16),
            pltpu.VMEM((reach, rows, dv), BF16),
            pltpu.VMEM((n, 2 * count, wide), BF16),
            pltpu.VMEM(((reach + 1) * rows, depth + EXTRA), BF16),
            pltpu.VMEM((dv + EXTRA, (reach + 1) * rows), BF16),
            pltpu.VMEM((n * count, depth + EXTRA), BF16),
            pltpu.VMEM((n // group, dv + EXTRA, chunk), BF16),
            pltpu.VMEM((heads // 2, dv + EXTRA, 2 * rows), F32),
            pltpu.VMEM((2, heads, rows), F32),
            pltpu.VMEM((rows * heads, dv), F32),
            pltpu.SemaphoreType.DMA((3,)),
            pltpu.SemaphoreType.DMA((2, reach)),
            pltpu.SemaphoreType.DMA((2, reach)),
            pltpu.SemaphoreType.DMA((n,)),
            pltpu.SemaphoreType.DMA((n,)),
        ],
        compiler_params=pltpu.CompilerParams(
            collective_id=0, has_side_effects=True, vmem_limit_bytes=61440 * 2**10
        ),
        cost_estimate=pl.CostEstimate(
            flops=flops, bytes_accessed=6 * 2**20, transcendentals=rows * heads * 768
        ),
    )(
        queries.transpose(1, 2, 0),
        keys.T,
        values,
        key_first.T,
        key_second,
        value_first,
        value_second,
        gate_table.T,
        gate_index.T,
    )


def solution(mesh):
    split = P(("sa", "sb"))
    inner = mesh.shape["sb"]
    n = mesh.shape["sa"] * inner
    return jax.shard_map(
        functools.partial(local, n, inner),
        mesh=mesh,
        in_specs=(split, split, split, P(), P(), P(), P(), P(), split),
        out_specs=split,
        check_vma=False,
    )
```

```python
import functools

import jax
import jax.numpy as jnp
from jax import lax
from jax.experimental import pallas as pl
from jax.experimental.pallas import tpu as pltpu
from jax.sharding import PartitionSpec as P

STRIDE = 16
WINDOW = 512
EXTRA = 16
NEG = -1e30
F32 = jnp.float32
BF16 = jnp.bfloat16


def dot(a, b):
    return jnp.dot(a, b, preferred_element_type=F32)


def silu(x):
    return x / (1.0 + jnp.exp(-x))


def kernel(
    n,
    inner,
    group,
    q_hbm,
    kt_ref,
    v_ref,
    w1k_hbm,
    w2k_ref,
    w1v_hbm,
    w2v_ref,
    table_ref,
    index_ref,
    out_ref,
    q_buf,
    w1k_buf,
    w1v_buf,
    kbuf,
    vbuf,
    gath,
    krows,
    vcols,
    crows,
    ccols,
    near,
    gates,
    out32,
    load_sem,
    halo_send,
    halo_recv,
    sum_send,
    sum_recv,
    edge_out,
    edge_in,
    edge_sem,
):
    heads, depth, rows = q_hbm.shape
    dv = v_ref.shape[1]
    reach = WINDOW // rows
    count = rows // STRIDE
    chunk = group * count
    chunks = n // group
    me = lax.axis_index("sa") * inner + lax.axis_index("sb")
    factor = depth ** (-0.5) * 1.4426950408889634

    def place(i):
        return (i // inner, i % inner)

    loads = [
        pltpu.make_async_copy(w1k_hbm, w1k_buf, load_sem.at[0]),
        pltpu.make_async_copy(w1v_hbm, w1v_buf, load_sem.at[1]),
        pltpu.make_async_copy(q_hbm, q_buf.at[:, pl.ds(0, depth), :], load_sem.at[2]),
    ]
    for load in loads:
        load.start()

    barrier = pltpu.get_barrier_semaphore()

    @pl.loop(0, me)
    def _(i):
        pl.semaphore_signal(
            barrier, inc=1, device_id=place(i), device_id_type=pl.DeviceIdType.MESH
        )

    token = lax.broadcasted_iota(jnp.int32, (EXTRA, rows), 1)
    line = lax.broadcasted_iota(jnp.int32, (EXTRA, rows), 0)
    marks = jnp.where((line == 0) | (line - 1 == (token + 1) // STRIDE), 1.0, 0.0).astype(BF16)
    for h in range(heads):
        q_buf[h, depth:, :] = marks
    for i in range(1, reach + 1):

        @pl.when(me < i)
        def _():
            kbuf[i - 1] = jnp.zeros(kbuf.shape[1:], BF16)
            vbuf[i - 1] = jnp.zeros(vbuf.shape[1:], BF16)

    @pl.when(me == 0)
    def _():
        edge_in[...] = jnp.zeros(edge_in.shape, F32)

    index = index_ref[...]
    for column in range(2):
        gate = jnp.zeros(index.shape, F32)
        for level in range(table_ref.shape[1]):
            gate = jnp.where(index == level, table_ref[column, level], gate)
        gates[column] = gate

    own_k = kt_ref[...]
    own_v = v_ref[...]
    lane = lax.broadcasted_iota(jnp.int32, (depth, rows), 1)
    zero_k = jnp.zeros_like(own_k)
    spread = jnp.concatenate(
        [jnp.where(lane % STRIDE == u, own_k, zero_k) for u in range(STRIDE)], axis=0
    )
    loads[0].wait()
    half = STRIDE * depth
    front_k, back_k = [
        jnp.sum(
            dot(w1k_buf[:, side * half : (side + 1) * half], spread).T.reshape(count, STRIDE, depth),
            axis=1,
        )
        for side in range(2)
    ]
    row = lax.broadcasted_iota(jnp.int32, (rows, dv), 0)
    zero_v = jnp.zeros_like(own_v)
    spread = jnp.concatenate(
        [jnp.where(row % STRIDE == u, own_v, zero_v) for u in range(STRIDE)], axis=1
    )
    loads[1].wait()
    half = STRIDE * dv
    front_v, back_v = [
        jnp.sum(
            dot(spread, w1v_buf[side * half : (side + 1) * half, :]).reshape(count, STRIDE, dv),
            axis=1,
        )
        for side in range(2)
    ]
    edge_out[:, :depth] = front_k
    edge_out[:, depth:256] = jnp.zeros((count, 256 - depth), F32)
    edge_out[:, 256:] = front_v

    @pl.when(me < n - 1)
    def _():
        pl.semaphore_wait(barrier, n - 1 - me)

    def edge_copy():
        return pltpu.make_async_remote_copy(
            src_ref=edge_out,
            dst_ref=edge_in,
            send_sem=edge_sem.at[0],
            recv_sem=edge_sem.at[1],
            device_id=place(jnp.minimum(me + 1, n - 1)),
            device_id_type=pl.DeviceIdType.MESH,
        )

    @pl.when(me < n - 1)
    def _():
        edge_copy().start()

    def halo(i):
        to = jnp.minimum(me + i, n - 1)
        return [
            pltpu.make_async_remote_copy(
                src_ref=src,
                dst_ref=dst.at[i - 1],
                send_sem=halo_send.at[part, i - 1],
                recv_sem=halo_recv.at[part, i - 1],
                device_id=place(to),
                device_id_type=pl.DeviceIdType.MESH,
            )
            for part, (src, dst) in enumerate([(kt_ref, kbuf), (v_ref, vbuf)])
        ]

    for i in range(1, reach + 1):

        @pl.when(me + i < n)
        def _():
            for copy in halo(i):
                copy.start()

    @pl.when(me >= 1)
    def _():
        edge_copy().wait_recv()

    def finish(own, fronts, incoming, second):
        row = lax.broadcasted_iota(jnp.int32, own.shape, 0)
        hidden = own + jnp.where(row == 0, pltpu.roll(incoming, 1, 0), pltpu.roll(fronts, 1, 0))
        return dot(silu(hidden).astype(BF16), second)

    before = edge_in[...]
    key_summary = finish(back_k, front_k, before[:, :depth], w2k_ref[...])
    value_summary = finish(back_v, front_v, before[:, 256 : 256 + dv], w2v_ref[...])
    wide = gath.shape[2]
    top = jnp.concatenate([key_summary, jnp.zeros((count, wide - depth), F32)], axis=1)
    bottom = jnp.concatenate([value_summary, jnp.zeros((count, wide - dv), F32)], axis=1)
    gath[me] = jnp.concatenate([top, bottom], axis=0).astype(BF16)

    def summary(source, to):
        return pltpu.make_async_remote_copy(
            src_ref=gath.at[source],
            dst_ref=gath.at[source],
            send_sem=sum_send.at[to],
            recv_sem=sum_recv.at[source],
            device_id=place(to),
            device_id_type=pl.DeviceIdType.MESH,
        )

    @pl.loop(me + 1, n)
    def _(to):
        summary(me, to).start()

    for i in range(1, reach + 1):

        @pl.when(me >= i)
        def _():
            for copy in halo(i):
                copy.wait_recv()

    first_lane = lax.broadcasted_iota(jnp.int32, (rows, EXTRA), 1) == 0
    for slot in range(reach + 1):
        i = reach - slot
        kt = own_k if i == 0 else kbuf[i - 1]
        vv = own_v if i == 0 else vbuf[i - 1]
        here = pl.ds(slot * rows, rows)
        krows[here, :depth] = kt.astype(F32).T.astype(BF16)
        krows[here, depth:] = jnp.where(first_lane & (me < i), NEG, 0.0).astype(BF16)
        vcols[:dv, here] = vv.astype(F32).T.astype(BF16)
    vcols[dv:, :] = jnp.ones((EXTRA, vcols.shape[1]), BF16)
    loads[2].wait()
    pair = 2 * rows
    within = lax.broadcasted_iota(jnp.int32, (rows, pair), 0) <= (
        lax.broadcasted_iota(jnp.int32, (rows, pair), 1) % rows
    )

    def queries(h):
        return jnp.concatenate([q_buf[2 * h], q_buf[2 * h + 1]], axis=1)

    @pl.loop(0, heads // 2, unroll=8)
    def _(h):
        scores = dot(krows[...], queries(h))
        edge = jnp.where(within, scores[reach * rows :], scores[:rows])
        kept = jnp.concatenate([edge, scores[rows : reach * rows]], axis=0)
        best = jnp.max(kept, axis=0, keepdims=True)
        weights = jnp.exp2(kept * factor - best * factor)
        old = jnp.where(within, 0.0, weights[:rows])
        new = jnp.where(within, weights[:rows], 0.0)
        full = jnp.concatenate([old, weights[rows:], new], axis=0).astype(BF16)
        near[h] = dot(vcols[...], full)

    @pl.loop(0, me)
    def _(source):
        summary(source, me).wait_recv()

    needed = me // group + 1

    def prepare(c, carry):
        whole = gath[pl.ds(c * group, group)].astype(F32)
        device = c * group + lax.broadcasted_iota(jnp.int32, (group, 2 * count, wide), 0)
        whole = jnp.where(device <= me, whole, 0.0)
        block = c * chunk + lax.broadcasted_iota(jnp.int32, (chunk, EXTRA), 0)
        column = lax.broadcasted_iota(jnp.int32, (chunk, EXTRA), 1)
        local = block - me * count
        hide = ((column == 0) & (local >= count)) | (
            (column >= 1) & (local >= 0) & (column - 1 <= local)
        )
        here = pl.ds(pl.multiple_of(c * chunk, chunk), chunk)
        crows[here, :depth] = whole[:, :count, :depth].reshape(chunk, depth).astype(BF16)
        crows[here, depth:] = jnp.where(hide, NEG, 0.0).astype(BF16)
        ccols[c, :dv, :] = whole[:, count:, :dv].reshape(chunk, dv).T.astype(BF16)
        ccols[c, dv:, :] = jnp.ones((EXTRA, chunk), BF16)
        return carry

    if chunks == 1:
        prepare(0, 0)
    else:
        lax.fori_loop(0, needed, prepare, 0)

    @pl.loop(0, heads // 2, unroll=8)
    def _(h):
        query = queries(h)

        def part(c):
            here = pl.ds(pl.multiple_of(c * chunk, chunk), chunk)
            scores = dot(crows[here, :], query)
            return scores, jnp.max(scores, axis=0, keepdims=True)

        def weigh(c, scores, best):
            return dot(ccols[c], jnp.exp2(scores * factor - best * factor).astype(BF16))

        if chunks == 1:
            scores, best = part(0)
            far = weigh(0, scores, jnp.maximum(best, 0.1 * NEG))
        else:

            def absorb(c, carry):
                best, total = carry
                scores, fresh = part(c)
                fresh = jnp.maximum(best, fresh)
                shrink = jnp.exp2(best * factor - fresh * factor)
                return fresh, total * shrink + weigh(c, scores, fresh)

            start = (jnp.full((1, pair), 0.1 * NEG, F32), jnp.zeros((dv + EXTRA, pair), F32))
            far = lax.fori_loop(0, needed, absorb, start)[1]
        local = near[h]
        gate = [
            jnp.concatenate([gates[c, pl.ds(2 * h, 1), :], gates[c, pl.ds(2 * h + 1, 1), :]], axis=1)
            for c in range(2)
        ]
        total = far[dv : dv + 1]
        seen = total > 0.0
        far_gate = jnp.where(seen, gate[0] / jnp.where(seen, total, 1.0), 0.0)
        near_gate = gate[1] / local[dv : dv + 1]
        mixed = far[:dv] * far_gate + local[:dv] * near_gate
        for side in range(2):
            out32[pl.ds(2 * h + side, rows, stride=heads), :] = mixed[
                :, side * rows : (side + 1) * rows
            ].T

    out_ref[...] = out32[...].reshape(rows, heads, dv).astype(BF16)

    for i in range(1, reach + 1):

        @pl.when(me + i < n)
        def _():
            for copy in halo(i):
                copy.wait_send()

    @pl.when(me < n - 1)
    def _():
        edge_copy().wait_send()

    @pl.loop(me + 1, n)
    def _(to):
        summary(me, to).wait_send()


def local(
    n,
    inner,
    queries,
    keys,
    values,
    key_first,
    key_second,
    value_first,
    value_second,
    gate_table,
    gate_index,
):
    rows, heads, depth = queries.shape
    dv = values.shape[1]
    reach = WINDOW // rows
    count = rows // STRIDE
    group = min(n, 256 // count)
    chunk = group * count
    wide = 256
    flops = 2 * rows * heads * (depth + dv) * (WINDOW + rows + n * count)
    vmem = pl.BlockSpec(memory_space=pltpu.VMEM)
    hbm = pl.BlockSpec(memory_space=pltpu.HBM)
    smem = pl.BlockSpec(memory_space=pltpu.SMEM)
    return pl.pallas_call(
        functools.partial(kernel, n, inner, group),
        out_shape=pltpu.VMEM((rows, heads, dv), BF16),
        in_specs=[hbm, vmem, vmem, hbm, vmem, hbm, vmem, smem, vmem],
        out_specs=vmem,
        scratch_shapes=[
            pltpu.VMEM((heads, depth + EXTRA, rows), BF16),
            pltpu.VMEM(key_first.shape[::-1], BF16),
            pltpu.VMEM(value_first.shape, BF16),
            pltpu.VMEM((reach, depth, rows), BF16),
            pltpu.VMEM((reach, rows, dv), BF16),
            pltpu.VMEM((n, 2 * count, wide), BF16),
            pltpu.VMEM(((reach + 1) * rows, depth + EXTRA), BF16),
            pltpu.VMEM((dv + EXTRA, (reach + 1) * rows), BF16),
            pltpu.VMEM((n * count, depth + EXTRA), BF16),
            pltpu.VMEM((n // group, dv + EXTRA, chunk), BF16),
            pltpu.VMEM((heads // 2, dv + EXTRA, 2 * rows), F32),
            pltpu.VMEM((2, heads, rows), F32),
            pltpu.VMEM((rows * heads, dv), F32),
            pltpu.SemaphoreType.DMA((3,)),
            pltpu.SemaphoreType.DMA((2, reach)),
            pltpu.SemaphoreType.DMA((2, reach)),
            pltpu.SemaphoreType.DMA((n,)),
            pltpu.SemaphoreType.DMA((n,)),
            pltpu.VMEM((count, 256 + dv), F32),
            pltpu.VMEM((count, 256 + dv), F32),
            pltpu.SemaphoreType.DMA((2,)),
        ],
        compiler_params=pltpu.CompilerParams(
            collective_id=0, has_side_effects=True, vmem_limit_bytes=61440 * 2**10
        ),
        cost_estimate=pl.CostEstimate(
            flops=flops, bytes_accessed=6 * 2**20, transcendentals=rows * heads * 768
        ),
    )(
        queries.transpose(1, 2, 0),
        keys.T,
        values,
        key_first.T,
        key_second,
        value_first,
        value_second,
        gate_table.T,
        gate_index.T,
    )


def solution(mesh):
    split = P(("sa", "sb"))
    inner = mesh.shape["sb"]
    n = mesh.shape["sa"] * inner
    return jax.shard_map(
        functools.partial(local, n, inner),
        mesh=mesh,
        in_specs=(split, split, split, P(), P(), P(), P(), P(), split),
        out_specs=split,
        check_vma=False,
    )
```
